256 devices in a mesh: seq: 64 (over z, x, core), grp: 4 (over y).
Axes of the slice: x: 4, y: 4, z: 8, core: 2. Of those that a mesh axis runs over, the one named last changes fastest.
Arguments:
- patches: bfloat16 [262144, 1024], P(('seq', 'grp')), may hold values from -6 to 6
- dest_map: int32 [256, 64], P(('seq', 'grp')), may hold values from 0 to 63, each once within a row
- series_ids: int32 [64, 64], P('seq'), may hold values from 0 to 15, never falling along the last dimension, each value on 1 to 32 neighbouring positions
- lengths: int32 [64, 64], P('seq'), may hold values from 1 to 64
- w_qkv: bfloat16 [1024, 3072], replicated
- w_out: bfloat16 [1024, 1024], replicated, may hold values from -0.1875 to 0.1875
- gain_var: float32 [1024], replicated, may hold values from 0.1 to 1.9
- gain_time: float32 [1024], replicated, may hold values from 0.1 to 1.9
Outputs:
- mixed: bfloat16 [262144, 1024], P(('seq', 'grp'))
The draws below stay inside these ranges and needn't reach their ends.
Inputs may be any that keep to these rules, and one draw needn't show every extreme that they name: Each row of dest_map names every index along seq once. `series_ids`: series numbers never fall along a pack's variate slots.
All inputs are finite; a program needn't handle non-finite values.
Results may differ from the reference program's by a relative error of at most 0.012.
Values may be sent and summed in bfloat16 or wider, within the bound.
A program may use at most 192 MiB of HBM per device.

```python
import math
import jax
import jax.numpy as jnp
import numpy as np
from jax import lax

D = 1024
HEADS = 16
TIME = 64
VAR = 64
ROWS = 262144
N_SEQ = 64
N_GRP = 4


def draw_w_qkv(key, part):
    first, second, third = jax.random.split(key, 3)
    scale = D ** (-0.5)
    query = jax.random.normal(first, (D, D), jnp.float32) * scale
    keys = jax.random.normal(second, (D, D), jnp.float32) * scale
    values = jax.random.normal(third, (D, D), jnp.float32) * scale
    return jnp.concatenate([query, keys, values], axis=1).astype(jnp.bfloat16)


def place_ends(drawn, stream_key, low, high):
    spot = [jax.random.randint(jax.random.fold_in(stream_key, axis), (), 0, length) for axis, length in enumerate(drawn.shape)]
    longest = drawn.shape.index(max(drawn.shape))
    next_to = spot[:longest] + [(spot[longest] + 1) % drawn.shape[longest]] + spot[longest + 1:]
    return drawn.at[tuple(spot)].set(low).at[tuple(next_to)].set(high)


def shard_levels(rng, shape, cuts, low, top_value):
    level = 1.0
    for dim, blocks in cuts:
        draws = jax.random.uniform(jax.random.fold_in(jax.random.fold_in(rng, 6), dim), (blocks,), jnp.float32, low / len(cuts), top_value / len(cuts))
        level = level * jnp.repeat(jnp.exp(draws), shape[dim] // blocks).reshape((-1,) + (1,) * (len(shape) - 1 - dim))
    return level


def profile(count, total, reach, slope):
    portions = [(1 << 20) // math.isqrt(standing ** slope) + 1 for standing in range(2, count + 1)]
    rest, holding = total - reach - (count - 1), [1] * (count - 1)
    while rest > 0:
        free = [i for i in range(count - 1) if holding[i] < reach]
        whole, remaining = sum([portions[i] for i in free]), rest
        for i in free:
            extra = min(reach - holding[i], max(1, remaining * portions[i] // whole), rest)
            holding[i] = holding[i] + extra
            rest = rest - extra
    return np.array([reach] + holding)


def ragged_sizes(own_key, count, total, limit, lean):
    if count == 2:
        one = jax.random.randint(own_key, (), max(1, total - limit), min(limit, total - 1) + 1)
        return jnp.stack([one, total - one])
    sizes = jnp.asarray(profile(count, total, limit, lean), jnp.int32)
    couples = (count - 1) // 2
    giver, taker = sizes[1:1 + 2 * couples:2], sizes[2:2 + 2 * couples:2]
    slack = jnp.minimum(giver - 1, limit - taker)
    passed = jax.random.randint(jax.random.fold_in(own_key, 1), (couples,), 0, 1 << 20) % (slack + 1)
    sizes = sizes.at[1:1 + 2 * couples:2].set(giver - passed).at[2:2 + 2 * couples:2].set(taker + passed)
    return sizes[jax.random.permutation(jax.random.fold_in(own_key, 2), count)]


def normal_values(stream_key, extent, deviation, limit, pieces=(), kind=jnp.bfloat16):
    array = deviation * jax.random.normal(stream_key, extent, jnp.float32)
    if pieces:
        array = array * shard_levels(stream_key, extent, pieces, -0.22, 0.18)
    return jnp.clip(array, -limit, limit).astype(kind)


def setup_inputs(seed: int = 0) -> dict:
    key_list = jax.random.split(jax.random.key(seed), 9)
    return {
        "patches": normal_values(key_list[0], (ROWS, D), 1.0, 6.0, ((0, 256),)),
        "dest_map": jax.vmap(lambda own: jax.random.permutation(own, N_SEQ))(jax.random.split(key_list[1], (N_SEQ * N_GRP))).reshape((N_SEQ * N_GRP, N_SEQ)).astype(jnp.int32),
        "series_ids": jax.vmap(lambda own: jnp.searchsorted(jnp.cumsum(ragged_sizes(own, VAR // 4, VAR, VAR // 2, 2)), jnp.arange(VAR), side="right"))(jax.random.split(key_list[2], N_SEQ)).reshape((N_SEQ, VAR)).astype(jnp.int32),
        "lengths": place_ends(jax.random.randint(key_list[3], (N_SEQ, VAR), 1, TIME + 1), jax.random.fold_in(key_list[3], 1), 1, TIME).astype(jnp.int32),
        "w_qkv": draw_w_qkv(jax.random.fold_in(key_list[8], 71), 0),
        "w_out": normal_values(key_list[5], (D, D), D ** -0.5, 0.1875),
        "gain_var": jnp.clip(1.0 + 0.18 * jax.random.normal(key_list[6], (D,), jnp.float32), 0.1, 1.9),
        "gain_time": jnp.clip(1.0 + 0.18 * jax.random.normal(key_list[7], (D,), jnp.float32), 0.1, 1.9),
    }


def rms_norm(values, gain):
    wide = values.astype(jnp.float32)
    scale = lax.rsqrt(lax.optimization_barrier(jnp.mean(wide * wide, axis=-1, keepdims=True)) + 1e-05)
    return (wide * scale * gain).astype(jnp.bfloat16)

def project(normed, w_qkv):
    first_dim, second_dim, width = normed.shape
    proj = jnp.dot(normed.reshape(first_dim * second_dim, width), w_qkv, preferred_element_type=jnp.float32).astype(jnp.bfloat16)
    proj = proj.reshape(first_dim, second_dim, 3, HEADS, width // HEADS)
    return (proj[:, :, 0], proj[:, :, 1], proj[:, :, 2])

def attend(query, keys, values, keep, form_scores, form_context, w_out):
    scores = jnp.einsum(form_scores, query.astype(jnp.float32), keys.astype(jnp.float32)) * query.shape[-1] ** (-0.5)
    scores = jnp.where(keep, scores, -1e+30)
    scores = scores - lax.optimization_barrier(jnp.max(scores, axis=-1, keepdims=True))
    expo = jnp.exp(scores)
    weights = (expo / lax.optimization_barrier(jnp.sum(expo, axis=-1, keepdims=True))).astype(jnp.bfloat16)
    context = jnp.einsum(form_context, weights.astype(jnp.float32), values.astype(jnp.float32)).astype(jnp.bfloat16)
    first_dim, second_dim = (context.shape[0], context.shape[1])
    flat = context.reshape(first_dim * second_dim, -1)
    return jnp.dot(flat, w_out, preferred_element_type=jnp.float32).reshape(first_dim, second_dim, -1)

def reference(patches, dest_map, series_ids, lengths, w_qkv, w_out, gain_var, gain_time):
    rows_dev = TIME // N_GRP * VAR
    block = rows_dev // N_SEQ
    blocks = patches.reshape(N_SEQ, N_GRP, N_SEQ, block, D)
    order = jnp.argsort(dest_map, axis=-1).astype(jnp.int32).reshape(N_SEQ, N_GRP, N_SEQ)
    sent = jnp.take_along_axis(blocks, order[:, :, :, None, None], axis=2)
    packed = jnp.transpose(sent, (2, 1, 0, 3, 4)).reshape(N_SEQ, TIME, VAR, D)

    def one_pack(items):
        pack, ids, lens = items
        same = (ids[:, None] == ids[None, :])[None, None, :, :]
        query, keys, values = project(rms_norm(pack, gain_var), w_qkv)
        branch = attend(query, keys, values, same, 'glhe,gmhe->ghlm', 'ghlm,gmhe->glhe', w_out)
        first = (pack.astype(jnp.float32) + branch).astype(jnp.bfloat16)
        query, keys, values = project(rms_norm(first, gain_time), w_qkv)
        valid = jnp.arange(TIME)[None, None, None, :] < lens[:, None, None, None]
        branch = attend(query, keys, values, valid, 'lghe,mghe->ghlm', 'ghlm,mghe->lghe', w_out)
        return (first.astype(jnp.float32) + branch).astype(jnp.bfloat16)
    mixed = lax.map(one_pack, (packed, series_ids, lengths))
    return mixed.reshape(N_SEQ * TIME * VAR, D)
```

```python
import functools
import math

import jax
import jax.numpy as jnp
from jax import lax
from jax.experimental import pallas as pl
from jax.experimental.pallas import tpu as pltpu
from jax.sharding import PartitionSpec as P

MESH = pl.DeviceIdType.MESH
BF16 = jnp.bfloat16
F32 = jnp.float32

WIDTH = 1024
ROW = 16
TILE = 256
COLS = 512
SCALE = 64**-0.5 * math.log2(math.e)


def hop(e):
    return jnp.where(e % 2 == 1, (e + 1) // 2, lax.rem(8 - e // 2, 8))


def one_hot(source_row):
    rows = lax.broadcasted_iota(jnp.int32, (TILE, TILE), 0)
    cols = lax.broadcasted_iota(jnp.int32, (TILE, TILE), 1)
    return jnp.where(rows == source_row(cols), 1.0, 0.0).astype(BF16)


def kernel(
    order_ref,
    patches_hbm,
    info_ref,
    wqkv_hbm,
    wout_hbm,
    gain_var_ref,
    gain_time_ref,
    out_hbm,
    patches,
    wqkv,
    wout,
    info,
    perms,
    outgoing,
    packed,
    spread,
    turned,
    back,
    landed,
    resid,
    normed,
    qkv,
    qkv_time,
    context,
    result,
    load_sem,
    info_sem,
    send1,
    recv1,
    send2,
    recv2,
    send3,
    recv3,
    out_sem,
):
    seq = lax.axis_index("seq")
    y = lax.axis_index("grp")
    z, x, c = seq // 8, lax.rem(seq // 2, 4), lax.rem(seq, 2)
    chip = z * 4 + x
    to_core = x // 2
    member = y * 2 + c

    loads = [
        pltpu.make_async_copy(patches_hbm, patches, load_sem.at[0]),
        pltpu.make_async_copy(wqkv_hbm, wqkv, load_sem.at[1]),
        pltpu.make_async_copy(wout_hbm, wout, load_sem.at[2]),
    ]
    for load in loads:
        load.start()

    barrier = pltpu.get_barrier_semaphore()

    @pl.loop(0, 32)
    def _(j):
        source = ((j // 4) * 4 + 2 * c + lax.rem(j // 2, 2)) * 2 + lax.rem(j, 2)

        @pl.when(source != seq)
        def _():
            pl.semaphore_signal(
                barrier, inc=1, device_id={"seq": source, "grp": y}, device_id_type=MESH
            )

    @pl.loop(1, 8)
    def _(j):
        pl.semaphore_signal(
            barrier,
            inc=1,
            device_id={
                "seq": chip * 2 + lax.rem(c + j, 2),
                "grp": lax.rem(y + j // 2, 4),
            },
            device_id_type=MESH,
        )

    perms[0] = one_hot(lambda r: (r % 64) * 4 + r // 64)
    perms[1] = one_hot(lambda r: ((r // 4) % 8) * 32 + (r // 32) * 4 + r % 4)

    def to_time(r):
        e = ((r // 32) % 2) * 4 + r % 4
        k = 2 * lax.rem(z - hop(e) + 8, 8) + (r // 4) % 2
        return ((r // 8) % 4) * 64 + k * 4 + r // 64

    perms[2] = one_hot(to_time)
    perms[3] = one_hot(lambda r: ((r // 4) % 4) * 64 + (r // 16) * 4 + r % 4)

    pl.semaphore_wait(barrier, 39 - jnp.where(to_core == c, 1, 0))
    loads[0].wait()

    info_local = pltpu.make_async_copy(info_ref, info.at[c], info_sem.at[0])
    info_remote = pltpu.make_async_remote_copy(
        src_ref=info_ref,
        dst_ref=info.at[c],
        send_sem=info_sem.at[1],
        recv_sem=info_sem.at[2],
        device_id={"seq": chip * 2 + 1 - c, "grp": y},
        device_id_type=MESH,
    )

    def place1(jj):
        e, dx, p = lax.rem(jj // 4, 8), lax.rem(jj, 4), jj // 32
        to_chip = lax.rem(z + hop(e), 8) * 4 + lax.rem(x + dx, 4)
        slot = p * 32 + e * 4 + lax.rem(x, 2) * 2 + c
        return to_chip, to_chip * 2 + to_core, p, slot

    def rows1(ref, slot):
        return ref.at[pl.ds(pl.multiple_of(slot * ROW, ROW), ROW)]

    def send_blocks(begin, end):
        @pl.loop(begin, end)
        def _(jj):
            to_chip, dest, p, slot = place1(jj)
            block = order_ref[to_chip * 2 + p]
            outgoing[jj] = patches[block]

            @pl.when(dest != seq)
            def _():
                pltpu.make_async_remote_copy(
                    src_ref=outgoing.at[jj],
                    dst_ref=rows1(packed, slot),
                    send_sem=send1.at[jj],
                    recv_sem=recv1.at[slot],
                    device_id={"seq": dest, "grp": y},
                    device_id_type=MESH,
                ).start()

            @pl.when(dest == seq)
            def _():
                pltpu.make_async_copy(
                    outgoing.at[jj], rows1(packed, slot), recv1.at[slot]
                ).start()

    send_blocks(0, 64)
    info_local.start()
    info_remote.start()

    lanes = lax.broadcasted_iota(jnp.int32, (64, 128), 1)
    first_half = lanes < 64
    diag_rows = lax.broadcasted_iota(jnp.int32, (128, 128), 0) // 64
    diag_cols = lax.broadcasted_iota(jnp.int32, (128, 128), 1) // 64
    ones = jnp.where(diag_rows == diag_cols, 1.0, 0.0).astype(BF16)
    pos = lax.broadcasted_iota(jnp.int32, (64, 128), 1) % 64
    key_time = (
        16 * ((pos // 8) % 4)
        + 2 * lax.rem(z - hop((pos // 32) * 4 + pos % 4) + 8, 8)
        + (pos // 4) % 2
    ).astype(F32)

    def norm(rows, gain_ref):
        wide = rows.astype(F32)
        mean = jnp.sum(wide * wide, axis=-1, keepdims=True) * (1.0 / WIDTH)
        normed[...] = (wide * lax.rsqrt(mean + 1e-05) * gain_ref[...]).astype(BF16)

    def attend(source, row, target, target_row, keep):
        zero = jnp.zeros((64, 128), BF16)
        rows = pl.ds(pl.multiple_of(row, 64), 64)
        for pair in range(8):
            query = source[rows, pair * 128 : pair * 128 + 128]
            keys = source[rows, WIDTH + pair * 128 : WIDTH + pair * 128 + 128]
            values = source[rows, 2 * WIDTH + pair * 128 : 2 * WIDTH + pair * 128 + 128]
            keys = jnp.concatenate(
                [jnp.where(first_half, keys, zero), jnp.where(first_half, zero, keys)], 0
            )
            values = jnp.concatenate(
                [jnp.where(first_half, values, zero), jnp.where(first_half, zero, values)], 0
            )
            scores = lax.dot_general(
                query, keys, (((1,), (1,)), ((), ())), preferred_element_type=F32
            )
            scores = jnp.where(keep, scores, -1e30)
            low = jnp.max(jnp.where(first_half, scores, -jnp.inf), axis=-1, keepdims=True)
            high = jnp.max(jnp.where(first_half, -jnp.inf, scores), axis=-1, keepdims=True)
            expo = jnp.exp2((scores - jnp.where(first_half, low, high)) * SCALE).astype(BF16)
            both = jnp.dot(
                expo, jnp.concatenate([values, ones], 1), preferred_element_type=F32
            )
            target[pl.ds(pl.multiple_of(target_row, 64), 64), pair * 128 : pair * 128 + 128] = (
                both[:, :128] / both[:, 128:]
            ).astype(BF16)

    def variates(p, q):
        at = p * 512 + q * TILE

        @pl.loop(0, 16)
        def _(j):
            slot = p * 32 + q * 16 + j
            pltpu.make_async_copy(
                rows1(packed, slot), rows1(packed, slot), recv1.at[slot]
            ).wait()

        norm(packed[at : at + TILE, :], gain_var_ref)

        @pl.loop(0, 3 * WIDTH // COLS)
        def _(n):
            cols = pl.ds(pl.multiple_of(n * COLS, COLS), COLS)
            qkv[:, cols] = jnp.dot(
                normed[...], wqkv[:, cols], preferred_element_type=F32
            ).astype(BF16)

        keep = info[p, :64, :] > 0.5

        @pl.loop(0, 4)
        def _(u):
            attend(qkv, u * 64, context, u * 64, keep)

        @pl.loop(0, WIDTH // COLS)
        def _(n):
            cols = pl.ds(pl.multiple_of(n * COLS, COLS), COLS)
            first = (
                jnp.dot(context[...], wout[:, cols], preferred_element_type=F32)
                + packed[at : at + TILE, cols].astype(F32)
            ).astype(BF16)
            spread[2 * p + q, :, cols] = jnp.dot(
                perms[0], first, preferred_element_type=F32
            ).astype(BF16)

        for j in range(8):
            dest_y, dest_c = lax.rem(y + j // 2, 4), lax.rem(c + j, 2)
            dest = dest_y * 2 + dest_c
            source = spread.at[2 * p + q, pl.ds(pl.multiple_of(dest * 32, 32), 32)]
            target = turned.at[2 * p + q, pl.ds(pl.multiple_of(member * 32, 32), 32)]
            if j == 0:
                pltpu.make_async_copy(source, target, recv2.at[2 * p + q, member]).start()
            else:
                pltpu.make_async_remote_copy(
                    src_ref=source,
                    dst_ref=target,
                    send_sem=send2.at[2 * p + q, j],
                    recv_sem=recv2.at[2 * p + q, member],
                    device_id={"seq": chip * 2 + dest_c, "grp": dest_y},
                    device_id_type=MESH,
                ).start()

    def project_time(p, q):
        @pl.loop(0, 8)
        def _(j):
            part = turned.at[2 * p + q, pl.ds(pl.multiple_of(j * 32, 32), 32)]
            pltpu.make_async_copy(part, part, recv2.at[2 * p + q, j]).wait()

        rows = jnp.dot(perms[1], turned[2 * p + q], preferred_element_type=F32).astype(BF16)
        for v in range(8):
            resid[v * 64 + q * 32 : v * 64 + q * 32 + 32, :] = rows[v * 32 : v * 32 + 32, :]
        norm(rows, gain_time_ref)

        @pl.loop(0, 3 * WIDTH // COLS)
        def _(n):
            cols = pl.ds(pl.multiple_of(n * COLS, COLS), COLS)
            proj = jnp.dot(normed[...], wqkv[:, cols], preferred_element_type=F32).astype(BF16)
            for v in range(8):
                qkv_time[v * 64 + q * 32 : v * 64 + q * 32 + 32, cols] = proj[
                    v * 32 : v * 32 + 32, :
                ]

    def times(p, h):
        @pl.loop(0, 4)
        def _(u):
            length = info[p, pl.ds(64 + member * 8 + h * 4 + u, 1), :]
            keep = key_time < jnp.broadcast_to(length, (64, 128))
            attend(qkv_time, h * TILE + u * 64, context, u * 64, keep)

        @pl.loop(0, WIDTH // COLS)
        def _(n):
            cols = pl.ds(pl.multiple_of(n * COLS, COLS), COLS)
            second = (
                jnp.dot(context[...], wout[:, cols], preferred_element_type=F32)
                + resid[h * TILE : h * TILE + TILE, cols].astype(F32)
            ).astype(BF16)
            second = jnp.dot(perms[2], second, preferred_element_type=F32).astype(BF16)
            back[2 * p + h, :, :, :, cols] = second.reshape(4, 4, ROW, COLS)

        for j in range(4):
            dest_y = lax.rem(y + j, 4)
            source = back.at[2 * p + h, dest_y]
            target = landed.at[:, member * 2 + h]

            def send():
                pltpu.make_async_remote_copy(
                    src_ref=source,
                    dst_ref=target,
                    send_sem=send3.at[2 * p + h, j],
                    recv_sem=recv3.at[member * 2 + h],
                    device_id={"seq": chip * 2 + p, "grp": dest_y},
                    device_id_type=MESH,
                ).start()

            if j == 0:
                pl.when(c != p)(send)

                @pl.when(c == p)
                def _():
                    pltpu.make_async_copy(source, target, recv3.at[member * 2 + h]).start()
            else:
                send()

    loads[1].wait()
    loads[2].wait()
    info_local.wait()
    info_remote.wait()

    variates(0, 0)
    variates(0, 1)
    project_time(0, 0)
    project_time(0, 1)
    times(0, 0)
    times(0, 1)
    variates(1, 0)
    variates(1, 1)
    project_time(1, 0)
    project_time(1, 1)
    times(1, 0)
    times(1, 1)

    @pl.loop(0, 16)
    def _(j):
        part = landed.at[:, j]
        pltpu.make_async_copy(part, part, recv3.at[j]).wait()

    writes = []
    for h in range(4):
        result[h * TILE : h * TILE + TILE, :] = jnp.dot(
            perms[3], landed[h].reshape(TILE, WIDTH), preferred_element_type=F32
        ).astype(BF16)
        rows = pl.ds(h * TILE, TILE)
        write = pltpu.make_async_copy(result.at[rows], out_hbm.at[rows], out_sem.at[h])
        write.start()
        writes.append(write)

    @pl.loop(0, 64)
    def _(jj):
        _, dest, _, _ = place1(jj)

        @pl.when(dest != seq)
        def _():
            pltpu.make_async_copy(outgoing.at[jj], outgoing.at[jj], send1.at[jj]).wait()

    for pq in range(4):
        for j in range(1, 8):
            part = spread.at[pq, pl.ds(0, 32)]
            pltpu.make_async_copy(part, part, send2.at[pq, j]).wait()
        for j in range(4):

            def drain():
                part = back.at[pq, j]
                pltpu.make_async_copy(part, part, send3.at[pq, j]).wait()

            if j == 0:
                pl.when(c != pq // 2)(drain)
            else:
                drain()

    for write in writes:
        write.wait()


def on_device(patches, dest_map, series_ids, lengths, w_qkv, w_out, gain_var, gain_time):
    index = jnp.arange(64, dtype=jnp.int32)
    order = jnp.sum(
        jnp.where(dest_map[0][None, :] == index[:, None], index[None, :], 0), axis=1
    ).astype(jnp.int32)
    ids = series_ids[0]
    same = (ids[:, None] == jnp.concatenate([ids, ids])[None, :]).astype(F32)
    valid = jnp.broadcast_to(lengths[0].astype(F32)[:, None], (64, 128))
    info = jnp.concatenate([same, valid], axis=0)
    any_space = pl.BlockSpec(memory_space=pl.ANY)
    vmem = pl.BlockSpec(memory_space=pltpu.VMEM)
    return pl.pallas_call(
        kernel,
        out_shape=jax.ShapeDtypeStruct((1024, WIDTH), BF16),
        in_specs=[
            pl.BlockSpec(memory_space=pltpu.SMEM),
            any_space,
            vmem,
            any_space,
            any_space,
            vmem,
            vmem,
        ],
        out_specs=any_space,
        scratch_shapes=[
            pltpu.VMEM((64, ROW, WIDTH), BF16),
            pltpu.VMEM((WIDTH, 3 * WIDTH), BF16),
            pltpu.VMEM((WIDTH, WIDTH), BF16),
            pltpu.VMEM((2, 128, 128), F32),
            pltpu.VMEM((4, TILE, TILE), BF16),
            pltpu.VMEM((64, ROW, WIDTH), BF16),
            pltpu.VMEM((1024, WIDTH), BF16),
            pltpu.VMEM((4, TILE, WIDTH), BF16),
            pltpu.VMEM((4, TILE, WIDTH), BF16),
            pltpu.VMEM((4, 4, 4, ROW, WIDTH), BF16),
            pltpu.VMEM((4, 16, ROW, WIDTH), BF16),
            pltpu.VMEM((512, WIDTH), BF16),
            pltpu.VMEM((TILE, WIDTH), BF16),
            pltpu.VMEM((TILE, 3 * WIDTH), BF16),
            pltpu.VMEM((512, 3 * WIDTH), BF16),
            pltpu.VMEM((TILE, WIDTH), BF16),
            pltpu.VMEM((1024, WIDTH), BF16),
            pltpu.SemaphoreType.DMA((3,)),
            pltpu.SemaphoreType.DMA((3,)),
            pltpu.SemaphoreType.DMA((64,)),
            pltpu.SemaphoreType.DMA((64,)),
            pltpu.SemaphoreType.DMA((4, 8)),
            pltpu.SemaphoreType.DMA((4, 8)),
            pltpu.SemaphoreType.DMA((4, 4)),
            pltpu.SemaphoreType.DMA((16,)),
            pltpu.SemaphoreType.DMA((4,)),
        ],
        compiler_params=pltpu.CompilerParams(
            collective_id=0, has_side_effects=True, vmem_limit_bytes=52 << 20
        ),
        cost_estimate=pl.CostEstimate(
            flops=20_000_000_000, bytes_accessed=12_000_000, transcendentals=4_000_000
        ),
        name="pack_layer",
    )(
        order,
        patches.reshape(64, ROW, WIDTH),
        info,
        w_qkv,
        w_out,
        gain_var.reshape(1, WIDTH),
        gain_time.reshape(1, WIDTH),
    )


def solution(mesh):
    return jax.shard_map(
        on_device,
        mesh=mesh,
        in_specs=(
            P(("seq", "grp"), None),
            P(("seq", "grp"), None),
            P("seq", None),
            P("seq", None),
            P(),
            P(),
            P(),
            P(),
        ),
        out_specs=P(("seq", "grp"), None),
        check_vma=False,
    )
```

```python
import functools
import math

import jax
import jax.numpy as jnp
from jax import lax
from jax.experimental import pallas as pl
from jax.experimental.pallas import tpu as pltpu
from jax.sharding import PartitionSpec as P

MESH = pl.DeviceIdType.MESH
BF16 = jnp.bfloat16
F32 = jnp.float32

WIDTH = 1024
ROW = 16
TILE = 256
COLS = 512
SCALE = 64**-0.5 * math.log2(math.e)


def hop(e):
    return jnp.where(e % 2 == 1, (e + 1) // 2, lax.rem(8 - e // 2, 8))


def one_hot(source_row):
    rows = lax.broadcasted_iota(jnp.int32, (TILE, TILE), 0)
    cols = lax.broadcasted_iota(jnp.int32, (TILE, TILE), 1)
    return jnp.where(rows == source_row(cols), 1.0, 0.0).astype(BF16)


def kernel(
    order_ref,
    patches_hbm,
    ids_hbm,
    lengths_hbm,
    wqkv_hbm,
    wout_hbm,
    gain_var_hbm,
    gain_time_hbm,
    landed,
    patches,
    small,
    gains,
    info_own,
    wqkv,
    wout,
    info,
    perms,
    outgoing,
    packed,
    spread,
    turned,
    back,
    resid,
    normed,
    qkv,
    qkv_time,
    context,
    load_sem,
    info_sem,
    send1,
    recv1,
    send2,
    recv2,
    send3,
    recv3,
):
    seq = lax.axis_index("seq")
    y = lax.axis_index("grp")
    z, x, c = seq // 8, lax.rem(seq // 2, 4), lax.rem(seq, 2)
    chip = z * 4 + x
    to_core = x // 2
    member = y * 2 + c

    loads = [
        pltpu.make_async_copy(patches_hbm, patches, load_sem.at[0]),
        pltpu.make_async_copy(ids_hbm, small.at[pl.ds(0, 1)], load_sem.at[1]),
        pltpu.make_async_copy(lengths_hbm, small.at[pl.ds(1, 1)], load_sem.at[2]),
        pltpu.make_async_copy(gain_var_hbm, gains.at[0], load_sem.at[3]),
        pltpu.make_async_copy(gain_time_hbm, gains.at[1], load_sem.at[4]),
        pltpu.make_async_copy(wqkv_hbm, wqkv, load_sem.at[5]),
        pltpu.make_async_copy(wout_hbm, wout, load_sem.at[6]),
    ]
    for load in loads:
        load.start()

    barrier = pltpu.get_barrier_semaphore()

    @pl.loop(0, 32)
    def _(j):
        source = ((j // 4) * 4 + 2 * c + lax.rem(j // 2, 2)) * 2 + lax.rem(j, 2)

        @pl.when(source != seq)
        def _():
            pl.semaphore_signal(
                barrier, inc=1, device_id={"seq": source, "grp": y}, device_id_type=MESH
            )

    @pl.loop(1, 8)
    def _(j):
        pl.semaphore_signal(
            barrier,
            inc=1,
            device_id={
                "seq": chip * 2 + lax.rem(c + j, 2),
                "grp": lax.rem(y + j // 2, 4),
            },
            device_id_type=MESH,
        )

    perms[0] = one_hot(lambda r: (r % 64) * 4 + r // 64)
    perms[1] = one_hot(lambda r: ((r // 4) % 8) * 32 + (r // 32) * 4 + r % 4)

    def to_time(r):
        e = ((r // 32) % 2) * 4 + r % 4
        k = 2 * lax.rem(z - hop(e) + 8, 8) + (r // 4) % 2
        return ((r // 8) % 4) * 64 + k * 4 + r // 64

    perms[2] = one_hot(to_time)

    pl.semaphore_wait(barrier, 39 - jnp.where(to_core == c, 1, 0))
    loads[0].wait()

    def place1(jj):
        e, dx, p = lax.rem(jj // 4, 8), lax.rem(jj, 4), jj // 32
        to_chip = lax.rem(z + hop(e), 8) * 4 + lax.rem(x + dx, 4)
        slot = p * 32 + e * 4 + lax.rem(x, 2) * 2 + c
        return to_chip, to_chip * 2 + to_core, p, slot

    def send_blocks(begin, end):
        @pl.loop(begin, end)
        def _(jj):
            to_chip, dest, p, slot = place1(jj)
            block = order_ref[to_chip * 2 + p]
            outgoing[jj] = patches[block]

            @pl.when(dest != seq)
            def _():
                pltpu.make_async_remote_copy(
                    src_ref=outgoing.at[jj],
                    dst_ref=packed.at[slot],
                    send_sem=send1.at[jj],
                    recv_sem=recv1.at[slot],
                    device_id={"seq": dest, "grp": y},
                    device_id_type=MESH,
                ).start()

            @pl.when(dest == seq)
            def _():
                pltpu.make_async_copy(
                    outgoing.at[jj], packed.at[slot], recv1.at[slot]
                ).start()

    send_blocks(0, 64)

    loads[1].wait()
    loads[2].wait()
    eye = lax.broadcasted_iota(jnp.int32, (64, 64), 0) == lax.broadcasted_iota(
        jnp.int32, (64, 64), 1
    )
    ids = small[0:1, :].astype(F32)
    ids_down = jnp.sum(jnp.where(eye, ids, 0.0), axis=1, keepdims=True)
    info_own[:64, :64] = jnp.where(ids_down == ids, 1.0, 0.0)
    info_own[:64, 64:] = jnp.where(ids_down == ids, 1.0, 0.0)
    count_down = jnp.sum(
        jnp.where(eye, small[1:2, :].astype(F32), 0.0), axis=1, keepdims=True
    )
    info_own[64:, :] = jnp.broadcast_to(count_down, (64, 128))
    info_local = pltpu.make_async_copy(info_own, info.at[c], info_sem.at[0])
    info_remote = pltpu.make_async_remote_copy(
        src_ref=info_own,
        dst_ref=info.at[c],
        send_sem=info_sem.at[1],
        recv_sem=info_sem.at[2],
        device_id={"seq": chip * 2 + 1 - c, "grp": y},
        device_id_type=MESH,
    )
    info_local.start()
    info_remote.start()

    lanes = lax.broadcasted_iota(jnp.int32, (64, 128), 1)
    first_half = lanes < 64
    diag_rows = lax.broadcasted_iota(jnp.int32, (128, 128), 0) // 64
    diag_cols = lax.broadcasted_iota(jnp.int32, (128, 128), 1) // 64
    ones = jnp.where(diag_rows == diag_cols, 1.0, 0.0).astype(BF16)
    pos = lax.broadcasted_iota(jnp.int32, (64, 128), 1) % 64
    key_time = (
        16 * ((pos // 8) % 4)
        + 2 * lax.rem(z - hop((pos // 32) * 4 + pos % 4) + 8, 8)
        + (pos // 4) % 2
    ).astype(F32)

    def norm(rows, gain):
        wide = rows.astype(F32)
        mean = jnp.sum(wide * wide, axis=-1, keepdims=True) * (1.0 / WIDTH)
        normed[...] = (wide * lax.rsqrt(mean + 1e-05) * gains[gain]).astype(BF16)

    zero = jnp.zeros((64, 128), BF16)

    def apart(pair):
        return jnp.concatenate(
            [jnp.where(first_half, pair, zero), jnp.where(first_half, zero, pair)], 0
        )

    def attend(source, begin, keeps):
        parts = [(u, pair * 128) for u in range(4) for pair in range(8)]
        expos = []
        scored = []
        for u, col in parts:
            rows = slice(begin + u * 64, begin + u * 64 + 64)
            scores = lax.dot_general(
                source[rows, col : col + 128],
                apart(source[rows, WIDTH + col : WIDTH + col + 128]),
                (((1,), (1,)), ((), ())),
                preferred_element_type=F32,
            )
            scored.append(jnp.where(keeps[u], scores, -1e30))
        for scores in scored:
            low = jnp.max(jnp.where(first_half, scores, -jnp.inf), axis=-1, keepdims=True)
            high = jnp.max(jnp.where(first_half, -jnp.inf, scores), axis=-1, keepdims=True)
            expos.append(
                jnp.exp2((scores - jnp.where(first_half, low, high)) * SCALE).astype(BF16)
            )
        for (u, col), expo in zip(parts, expos):
            rows = slice(begin + u * 64, begin + u * 64 + 64)
            values = apart(source[rows, 2 * WIDTH + col : 2 * WIDTH + col + 128])
            both = jnp.dot(
                expo, jnp.concatenate([values, ones], 1), preferred_element_type=F32
            )
            context[u * 64 : u * 64 + 64, col : col + 128] = (
                both[:, :128] / both[:, 128:]
            ).astype(BF16)

    def variates(p, q):
        @pl.loop(0, 16)
        def _(j):
            slot = p * 32 + q * 16 + j
            pltpu.make_async_copy(packed.at[slot], packed.at[slot], recv1.at[slot]).wait()

        blocks = pl.ds(pl.multiple_of(p * 32 + q * 16, 16), 16)
        norm(packed[blocks].reshape(TILE, WIDTH), 0)
        for col in range(0, 3 * WIDTH, COLS):
            cols = slice(col, col + COLS)
            qkv[:, cols] = jnp.dot(
                normed[...], wqkv[:, cols], preferred_element_type=F32
            ).astype(BF16)
        keep = info[p, :64, :] > 0.5
        attend(qkv, 0, [keep] * 4)
        for col in range(0, WIDTH, COLS):
            cols = slice(col, col + COLS)
            normed[:, cols] = (
                jnp.dot(context[...], wout[:, cols], preferred_element_type=F32)
                + packed[blocks, :, cols].reshape(TILE, COLS).astype(F32)
            ).astype(BF16)
        for col in range(0, WIDTH, COLS):
            cols = slice(col, col + COLS)
            spread[2 * p + q, :, cols] = jnp.dot(
                perms[0], normed[:, cols], preferred_element_type=F32
            ).astype(BF16)

        for j in range(8):
            dest_y, dest_c = lax.rem(y + j // 2, 4), lax.rem(c + j, 2)
            dest = dest_y * 2 + dest_c
            source = spread.at[2 * p + q, pl.ds(pl.multiple_of(dest * 32, 32), 32)]
            target = turned.at[2 * p + q, pl.ds(pl.multiple_of(member * 32, 32), 32)]
            if j == 0:
                pltpu.make_async_copy(source, target, recv2.at[2 * p + q, member]).start()
            else:
                pltpu.make_async_remote_copy(
                    src_ref=source,
                    dst_ref=target,
                    send_sem=send2.at[2 * p + q, j],
                    recv_sem=recv2.at[2 * p + q, member],
                    device_id={"seq": chip * 2 + dest_c, "grp": dest_y},
                    device_id_type=MESH,
                ).start()

    def project_time(p, q):
        @pl.loop(0, 8)
        def _(j):
            part = turned.at[2 * p + q, pl.ds(pl.multiple_of(j * 32, 32), 32)]
            pltpu.make_async_copy(part, part, recv2.at[2 * p + q, j]).wait()

        rows = jnp.dot(perms[1], turned[2 * p + q], preferred_element_type=F32).astype(BF16)
        for v in range(8):
            resid[v * 64 + q * 32 : v * 64 + q * 32 + 32, :] = rows[v * 32 : v * 32 + 32, :]
        norm(rows, 1)

        for col in range(0, 3 * WIDTH, COLS):
            cols = slice(col, col + COLS)
            proj = jnp.dot(normed[...], wqkv[:, cols], preferred_element_type=F32).astype(BF16)
            for v in range(8):
                qkv_time[v * 64 + q * 32 : v * 64 + q * 32 + 32, cols] = proj[
                    v * 32 : v * 32 + 32, :
                ]

    def times(p, h):
        keeps = []
        for u in range(4):
            length = info[p, pl.ds(64 + member * 8 + h * 4 + u, 1), :]
            keeps.append(key_time < jnp.broadcast_to(length, (64, 128)))
        attend(qkv_time, h * TILE, keeps)
        for col in range(0, WIDTH, COLS):
            cols = slice(col, col + COLS)
            normed[:, cols] = (
                jnp.dot(context[...], wout[:, cols], preferred_element_type=F32)
                + resid[h * TILE : h * TILE + TILE, cols].astype(F32)
            ).astype(BF16)
        for col in range(0, WIDTH, COLS):
            cols = slice(col, col + COLS)
            second = jnp.dot(perms[2], normed[:, cols], preferred_element_type=F32).astype(BF16)
            back[2 * p + h, :, :, :, cols] = second.reshape(4, 4, ROW, COLS)

        for j in range(4):
            dest_y = lax.rem(y + j, 4)
            source = back.at[2 * p + h, dest_y]
            target = landed.at[:, member * 2 + h]

            def send():
                pltpu.make_async_remote_copy(
                    src_ref=source,
                    dst_ref=target,
                    send_sem=send3.at[2 * p + h, j],
                    recv_sem=recv3.at[member * 2 + h],
                    device_id={"seq": chip * 2 + p, "grp": dest_y},
                    device_id_type=MESH,
                ).start()

            if j == 0:
                pl.when(c != p)(send)

                @pl.when(c == p)
                def _():
                    pltpu.make_async_copy(source, target, recv3.at[member * 2 + h]).start()
            else:
                send()

    for load in loads[3:]:
        load.wait()
    info_local.wait()
    info_remote.wait()

    @pl.loop(0, 2)
    def _(p):
        variates(p, 0)
        variates(p, 1)
        project_time(p, 0)
        project_time(p, 1)
        times(p, 0)
        times(p, 1)

    @pl.loop(0, 16)
    def _(j):
        part = landed.at[:, j]
        pltpu.make_async_copy(part, part, recv3.at[j]).wait()

    @pl.loop(0, 64)
    def _(jj):
        _, dest, _, _ = place1(jj)

        @pl.when(dest != seq)
        def _():
            pltpu.make_async_copy(outgoing.at[jj], outgoing.at[jj], send1.at[jj]).wait()

    for pq in range(4):
        for j in range(1, 8):
            part = spread.at[pq, pl.ds(0, 32)]
            pltpu.make_async_copy(part, part, send2.at[pq, j]).wait()
        for j in range(4):

            def drain():
                part = back.at[pq, j]
                pltpu.make_async_copy(part, part, send3.at[pq, j]).wait()

            if j == 0:
                pl.when(c != pq // 2)(drain)
            else:
                drain()


def in_time_order(landed_ref, out_hbm, result, sems):
    perm = one_hot(lambda r: ((r // 4) % 4) * 64 + (r // 16) * 4 + r % 4)
    writes = []
    for h in range(4):
        rows = pl.ds(h * TILE, TILE)
        result[rows, :] = jnp.dot(
            perm, landed_ref[h].reshape(TILE, WIDTH), preferred_element_type=F32
        ).astype(BF16)
        writes.append(pltpu.make_async_copy(result.at[rows], out_hbm.at[rows], sems.at[h]))
        writes[-1].start()
    for write in writes:
        write.wait()


def on_device(patches, dest_map, series_ids, lengths, w_qkv, w_out, gain_var, gain_time):
    index = jnp.arange(64, dtype=jnp.int32)
    order = jnp.sum(
        jnp.where(dest_map[0][None, :] == index[:, None], index[None, :], 0), axis=1
    ).astype(jnp.int32)
    any_space = pl.BlockSpec(memory_space=pl.ANY)
    landed = pl.pallas_call(
        kernel,
        out_shape=pltpu.VMEM((4, 16, ROW, WIDTH), BF16),
        in_specs=[pl.BlockSpec(memory_space=pltpu.SMEM)] + [any_space] * 7,
        out_specs=pl.BlockSpec(memory_space=pltpu.VMEM),
        scratch_shapes=[
            pltpu.VMEM((64, ROW, WIDTH), BF16),
            pltpu.VMEM((8, 64), jnp.int32),
            pltpu.VMEM((2, 1, WIDTH), F32),
            pltpu.VMEM((128, 128), F32),
            pltpu.VMEM((WIDTH, 3 * WIDTH), BF16),
            pltpu.VMEM((WIDTH, WIDTH), BF16),
            pltpu.VMEM((2, 128, 128), F32),
            pltpu.VMEM((3, TILE, TILE), BF16),
            pltpu.VMEM((64, ROW, WIDTH), BF16),
            pltpu.VMEM((64, ROW, WIDTH), BF16),
            pltpu.VMEM((4, TILE, WIDTH), BF16),
            pltpu.VMEM((4, TILE, WIDTH), BF16),
            pltpu.VMEM((4, 4, 4, ROW, WIDTH), BF16),
            pltpu.VMEM((512, WIDTH), BF16),
            pltpu.VMEM((TILE, WIDTH), BF16),
            pltpu.VMEM((TILE, 3 * WIDTH), BF16),
            pltpu.VMEM((512, 3 * WIDTH), BF16),
            pltpu.VMEM((TILE, WIDTH), BF16),
            pltpu.SemaphoreType.DMA((7,)),
            pltpu.SemaphoreType.DMA((3,)),
            pltpu.SemaphoreType.DMA((64,)),
            pltpu.SemaphoreType.DMA((64,)),
            pltpu.SemaphoreType.DMA((4, 8)),
            pltpu.SemaphoreType.DMA((4, 8)),
            pltpu.SemaphoreType.DMA((4, 4)),
            pltpu.SemaphoreType.DMA((16,)),
        ],
        compiler_params=pltpu.CompilerParams(
            collective_id=0, has_side_effects=True, vmem_limit_bytes=52 << 20
        ),
        cost_estimate=pl.CostEstimate(
            flops=20_000_000_000, bytes_accessed=12_000_000, transcendentals=4_000_000
        ),
        name="pack_layer",
    )(
        order,
        patches.reshape(64, ROW, WIDTH),
        series_ids,
        lengths,
        w_qkv,
        w_out,
        gain_var.reshape(1, WIDTH),
        gain_time.reshape(1, WIDTH),
    )
    return pl.pallas_call(
        in_time_order,
        out_shape=jax.ShapeDtypeStruct((1024, WIDTH), BF16),
        in_specs=[pl.BlockSpec(memory_space=pltpu.VMEM)],
        out_specs=any_space,
        scratch_shapes=[pltpu.VMEM((1024, WIDTH), BF16), pltpu.SemaphoreType.DMA((4,))],
        compiler_params=pltpu.CompilerParams(vmem_limit_bytes=8 << 20),
        name="time_order",
    )(landed)


def solution(mesh):
    return jax.shard_map(
        on_device,
        mesh=mesh,
        in_specs=(
            P(("seq", "grp"), None),
            P(("seq", "grp"), None),
            P("seq", None),
            P("seq", None),
            P(),
            P(),
            P(),
            P(),
        ),
        out_specs=P(("seq", "grp"), None),
        check_vma=False,
    )
```

```python
import functools
import math

import jax
import jax.numpy as jnp
from jax import lax
from jax.experimental import pallas as pl
from jax.experimental.pallas import tpu as pltpu
from jax.sharding import PartitionSpec as P

MESH = pl.DeviceIdType.MESH
BF16 = jnp.bfloat16
F32 = jnp.float32

WIDTH = 1024
ROW = 16
TILE = 256
COLS = 512
SCALE = 64**-0.5 * math.log2(math.e)


PARTNERS = ((0, 0), (1, 0), (3, 1), (1, 1), (3, 0), (2, 0), (2, 1), (0, 1))
CHUNKS = ((0, 4), (4, 2), (6, 2))


def hop(e):
    return jnp.where((e & 1) == 1, (e + 1) >> 1, (8 - (e >> 1)) & 7)


def hop_scalar(e):
    return jnp.where(e % 2 == 1, (e + 1) // 2, lax.rem(8 - e // 2, 8))


def one_hot(size, target):
    rows = lax.broadcasted_iota(jnp.int32, (size, size), 0)
    cols = lax.broadcasted_iota(jnp.int32, (1, size), 1)
    return jnp.where(rows == target(cols), 1.0, 0.0).astype(BF16)


def kernel(
    patches_hbm,
    dest_hbm,
    ids_hbm,
    lengths_hbm,
    wqkv_hbm,
    wout_hbm,
    gain_var_hbm,
    gain_time_hbm,
    landed,
    patches,
    small,
    gains,
    info_own,
    order_down,
    order_ref,
    wqkv,
    wout,
    info,
    perms,
    perms_half,
    outgoing,
    packed,
    spread,
    turned,
    back,
    resid,
    normed,
    qkv,
    qkv_time,
    context,
    load_sem,
    info_sem,
    send1,
    recv1,
    send2,
    recv2,
    send3,
    recv3,
):
    seq = lax.axis_index("seq")
    y = lax.axis_index("grp")
    z, x, c = seq // 8, lax.rem(seq // 2, 4), lax.rem(seq, 2)
    chip = z * 4 + x
    to_core = x // 2
    member = y * 2 + c

    loads = [
        pltpu.make_async_copy(patches_hbm, patches, load_sem.at[0]),
        pltpu.make_async_copy(dest_hbm, small.at[pl.ds(2, 1)], load_sem.at[1]),
        pltpu.make_async_copy(ids_hbm, small.at[pl.ds(0, 1)], load_sem.at[2]),
        pltpu.make_async_copy(lengths_hbm, small.at[pl.ds(1, 1)], load_sem.at[3]),
        pltpu.make_async_copy(gain_var_hbm, gains.at[0], load_sem.at[4]),
        pltpu.make_async_copy(gain_time_hbm, gains.at[1], load_sem.at[5]),
        pltpu.make_async_copy(wqkv_hbm, wqkv, load_sem.at[6]),
        pltpu.make_async_copy(wout_hbm, wout, load_sem.at[7]),
    ]
    for load in loads[:4]:
        load.start()

    barrier = pltpu.get_barrier_semaphore()

    @pl.loop(0, 32)
    def _(j):
        source = ((j // 4) * 4 + 2 * c + lax.rem(j // 2, 2)) * 2 + lax.rem(j, 2)

        @pl.when(source != seq)
        def _():
            pl.semaphore_signal(
                barrier, inc=1, device_id={"seq": source, "grp": y}, device_id_type=MESH
            )

    @pl.loop(1, 8)
    def _(j):
        pl.semaphore_signal(
            barrier,
            inc=1,
            device_id={
                "seq": chip * 2 + lax.rem(c + j, 2),
                "grp": lax.rem(y + j // 2, 4),
            },
            device_id_type=MESH,
        )

    eye = lax.broadcasted_iota(jnp.int32, (64, 64), 0) == lax.broadcasted_iota(
        jnp.int32, (64, 64), 1
    )

    def down(row):
        return jnp.sum(jnp.where(eye, row.astype(F32), 0.0), axis=1, keepdims=True)

    loads[1].wait()
    pack = lax.broadcasted_iota(jnp.int32, (64, 64), 1).astype(F32)
    number = lax.broadcasted_iota(jnp.int32, (64, 64), 0)
    order = jnp.sum(
        jnp.where(down(small[2:3, :]) == pack, number, 0), axis=0, keepdims=True
    )
    order_down[...] = jnp.minimum(order, 63)
    to_scalars = pltpu.make_async_copy(order_down, order_ref, load_sem.at[8])
    to_scalars.start()

    pl.semaphore_wait(barrier, 39 - jnp.where(to_core == c, 1, 0))
    to_scalars.wait()
    loads[0].wait()
    for load in loads[4:]:
        load.start()

    def place1(jj):
        e, dx, p = lax.rem(jj // 4, 8), lax.rem(jj, 4), jj // 32
        to_chip = lax.rem(z + hop_scalar(e), 8) * 4 + lax.rem(x + dx, 4)
        slot = p * 32 + e * 4 + lax.rem(x, 2) * 2 + c
        return to_chip, to_chip * 2 + to_core, p, slot

    def send_blocks(begin, end):
        @pl.loop(begin, end)
        def _(jj):
            to_chip, dest, p, slot = place1(jj)
            block = jnp.minimum(order_ref[0, to_chip * 2 + p], 63)
            outgoing[jj] = patches[block]

            @pl.when(dest != seq)
            def _():
                pltpu.make_async_remote_copy(
                    src_ref=outgoing.at[jj],
                    dst_ref=packed.at[slot],
                    send_sem=send1.at[jj],
                    recv_sem=recv1.at[slot],
                    device_id={"seq": dest, "grp": y},
                    device_id_type=MESH,
                ).start()

            @pl.when(dest == seq)
            def _():
                pltpu.make_async_copy(
                    outgoing.at[jj], packed.at[slot], recv1.at[slot]
                ).start()

    send_blocks(0, 64)

    loads[2].wait()
    loads[3].wait()
    ids = small[0:1, :].astype(F32)
    same = jnp.where(down(small[0:1, :]) == ids, 1.0, 0.0)
    info_own[:64, :64] = same
    info_own[:64, 64:] = same
    info_own[64:, :] = jnp.broadcast_to(down(small[1:2, :]), (64, 128))
    info_local = pltpu.make_async_copy(info_own, info.at[c], info_sem.at[0])
    info_remote = pltpu.make_async_remote_copy(
        src_ref=info_own,
        dst_ref=info.at[c],
        send_sem=info_sem.at[1],
        recv_sem=info_sem.at[2],
        device_id={"seq": chip * 2 + 1 - c, "grp": y},
        device_id_type=MESH,
    )
    info_local.start()
    info_remote.start()

    def by_variate(times):
        return lambda r: (r & 63) * times + (r >> 6)

    def gathered(shift):
        return lambda r: (
            (((r >> shift) & 7) << (3 + shift))
            + ((r >> (3 + shift)) << shift)
            + (r & ((1 << shift) - 1))
        )

    def sent(pos):
        early = pos < 32
        e = jnp.where(early, pos & 3, 4 + ((pos >> 4) & 1) * 2 + (pos & 1))
        sender = jnp.where(early, pos >> 2, (pos & 15) >> 1)
        return sender, 2 * ((z - hop(e) + 8) & 7) + (sender & 1)

    def to_time(r):
        sender, k = sent(r & 63)
        return (sender >> 1) * 64 + k * 4 + (r >> 6)

    perms[0] = one_hot(TILE, by_variate(4))
    perms[1] = one_hot(TILE, gathered(2))
    perms[2] = one_hot(TILE, to_time)
    perms_half[0] = one_hot(TILE // 2, by_variate(2))
    perms_half[1] = one_hot(TILE // 2, gathered(1))

    lanes = lax.broadcasted_iota(jnp.int32, (64, 128), 1)
    first_half = lanes < 64
    diag_rows = lax.broadcasted_iota(jnp.int32, (128, 128), 0) // 64
    diag_cols = lax.broadcasted_iota(jnp.int32, (128, 128), 1) // 64
    ones = jnp.where(diag_rows == diag_cols, 1.0, 0.0).astype(BF16)
    key_sender, key_k = sent(lanes & 63)
    key_time = (16 * (key_sender >> 1) + key_k).astype(F32)

    def norm(rows, gain):
        size = rows.shape[0]
        wide = rows.astype(F32)
        mean = jnp.sum(wide * wide, axis=-1, keepdims=True) * (1.0 / WIDTH)
        normed[:size] = (wide * lax.rsqrt(mean + 1e-05) * gains[gain]).astype(BF16)

    zero = jnp.zeros((64, 128), BF16)

    def apart(pair):
        return jnp.concatenate(
            [jnp.where(first_half, pair, zero), jnp.where(first_half, zero, pair)], 0
        )

    def attend(source, begin, keeps):
        parts = [(u, pair * 128) for u in range(len(keeps)) for pair in range(8)]
        expos = []
        scored = []
        for u, col in parts:
            rows = slice(begin + u * 64, begin + u * 64 + 64)
            scores = lax.dot_general(
                source[rows, col : col + 128],
                apart(source[rows, WIDTH + col : WIDTH + col + 128]),
                (((1,), (1,)), ((), ())),
                preferred_element_type=F32,
            )
            scored.append(jnp.where(keeps[u], scores, -1e30))
        for scores in scored:
            low = jnp.max(jnp.where(first_half, scores, -jnp.inf), axis=-1, keepdims=True)
            high = jnp.max(jnp.where(first_half, -jnp.inf, scores), axis=-1, keepdims=True)
            expos.append(
                jnp.exp2((scores - jnp.where(first_half, low, high)) * SCALE).astype(BF16)
            )
        for (u, col), expo in zip(parts, expos):
            rows = slice(begin + u * 64, begin + u * 64 + 64)
            values = apart(source[rows, 2 * WIDTH + col : 2 * WIDTH + col + 128])
            both = jnp.dot(
                expo, jnp.concatenate([values, ones], 1), preferred_element_type=F32
            )
            context[u * 64 : u * 64 + 64, col : col + 128] = (
                both[:, :128] / both[:, 128:]
            ).astype(BF16)

    def variates(p, q):
        begin, count = CHUNKS[q]
        size = count * 64

        @pl.loop(0, count * 4)
        def _(j):
            slot = p * 32 + begin * 4 + j
            pltpu.make_async_copy(packed.at[slot], packed.at[slot], recv1.at[slot]).wait()

        blocks = pl.ds(pl.multiple_of(p * 32 + begin * 4, 4), count * 4)
        norm(packed[blocks].reshape(size, WIDTH), 0)
        for col in range(0, 3 * WIDTH, COLS):
            cols = slice(col, col + COLS)
            qkv[:size, cols] = jnp.dot(
                normed[:size], wqkv[:, cols], preferred_element_type=F32
            ).astype(BF16)
        keep = info[p, :64, :] > 0.5
        attend(qkv, 0, [keep] * count)
        for col in range(0, WIDTH, COLS):
            cols = slice(col, col + COLS)
            normed[:size, cols] = (
                jnp.dot(context[:size], wout[:, cols], preferred_element_type=F32)
                + packed[blocks, :, cols].reshape(size, COLS).astype(F32)
            ).astype(BF16)
        perm = perms[0] if count == 4 else perms_half[0]
        for col in range(0, WIDTH, COLS):
            cols = slice(col, col + COLS)
            spread[p, begin * 64 : begin * 64 + size, cols] = jnp.dot(
                perm, normed[:size, cols], preferred_element_type=F32
            ).astype(BF16)
        part = count * 8
        for j, (dy, dc) in enumerate(PARTNERS):
            dest_y, dest_c = lax.rem(y + dy, 4), lax.rem(c + dc, 2)
            dest = dest_y * 2 + dest_c
            source = spread.at[p, pl.ds(pl.multiple_of(begin * 64 + dest * part, 16), part)]
            target = turned.at[p, pl.ds(pl.multiple_of(begin * 64 + member * part, 16), part)]
            if j == 0:
                pltpu.make_async_copy(source, target, recv2.at[p, q, member]).start()
            else:
                pltpu.make_async_remote_copy(
                    src_ref=source,
                    dst_ref=target,
                    send_sem=send2.at[p, q, j],
                    recv_sem=recv2.at[p, q, member],
                    device_id={"seq": chip * 2 + dest_c, "grp": dest_y},
                    device_id_type=MESH,
                ).start()

    def project_time(p, q):
        begin, count = CHUNKS[q]
        size, part = count * 64, count * 8

        @pl.loop(0, 8)
        def _(j):
            piece = turned.at[p, pl.ds(pl.multiple_of(begin * 64 + j * part, 16), part)]
            pltpu.make_async_copy(piece, piece, recv2.at[p, q, j]).wait()

        perm = perms[1] if count == 4 else perms_half[1]
        rows = jnp.dot(
            perm, turned[p, begin * 64 : begin * 64 + size], preferred_element_type=F32
        ).astype(BF16)
        for v in range(8):
            at = v * 64 + begin * 8
            resid[p, at : at + part, :] = rows[v * part : v * part + part, :]
        norm(rows, 1)
        for col in range(0, 3 * WIDTH, COLS):
            cols = slice(col, col + COLS)
            proj = jnp.dot(
                normed[:size], wqkv[:, cols], preferred_element_type=F32
            ).astype(BF16)
            for v in range(8):
                at = v * 64 + begin * 8
                qkv_time[p, at : at + part, cols] = proj[v * part : v * part + part, :]

    def times(p, h):
        keeps = []
        for u in range(4):
            length = info[p, pl.ds(64 + member * 8 + h * 4 + u, 1), :]
            keeps.append(key_time < jnp.broadcast_to(length, (64, 128)))
        attend(qkv_time.at[p], h * TILE, keeps)
        for col in range(0, WIDTH, COLS):
            cols = slice(col, col + COLS)
            normed[:, cols] = (
                jnp.dot(context[...], wout[:, cols], preferred_element_type=F32)
                + resid[p, h * TILE : h * TILE + TILE, cols].astype(F32)
            ).astype(BF16)
        for col in range(0, WIDTH, COLS):
            cols = slice(col, col + COLS)
            second = jnp.dot(perms[2], normed[:, cols], preferred_element_type=F32).astype(BF16)
            back[2 * p + h, :, :, :, cols] = second.reshape(4, 4, ROW, COLS)

        for j in (1, 3, 2, 0):
            dest_y = lax.rem(y + j, 4)
            source = back.at[2 * p + h, dest_y]
            target = landed.at[:, member * 2 + h]

            def send():
                pltpu.make_async_remote_copy(
                    src_ref=source,
                    dst_ref=target,
                    send_sem=send3.at[2 * p + h, j],
                    recv_sem=recv3.at[member * 2 + h],
                    device_id={"seq": chip * 2 + p, "grp": dest_y},
                    device_id_type=MESH,
                ).start()

            if j == 0:
                pl.when(c != p)(send)

                @pl.when(c == p)
                def _():
                    pltpu.make_async_copy(source, target, recv3.at[member * 2 + h]).start()
            else:
                send()

    for load in loads[4:]:
        load.wait()
    info_local.wait()
    info_remote.wait()

    variates(0, 0)
    project_time(0, 0)
    variates(0, 1)
    variates(0, 2)
    project_time(0, 1)
    project_time(0, 2)
    times(0, 0)
    variates(1, 0)
    variates(1, 1)
    variates(1, 2)
    times(0, 1)
    project_time(1, 0)
    project_time(1, 1)
    project_time(1, 2)
    times(1, 0)
    times(1, 1)

    @pl.loop(0, 16)
    def _(j):
        part = landed.at[:, j]
        pltpu.make_async_copy(part, part, recv3.at[j]).wait()

    @pl.loop(0, 64)
    def _(jj):
        _, dest, _, _ = place1(jj)

        @pl.when(dest != seq)
        def _():
            pltpu.make_async_copy(outgoing.at[jj], outgoing.at[jj], send1.at[jj]).wait()

    for p in range(2):
        for q, (_, count) in enumerate(CHUNKS):
            for j in range(1, 8):
                part = spread.at[p, pl.ds(0, count * 8)]
                pltpu.make_async_copy(part, part, send2.at[p, q, j]).wait()
    for pq in range(4):
        for j in range(4):

            def drain():
                part = back.at[pq, j]
                pltpu.make_async_copy(part, part, send3.at[pq, j]).wait()

            if j == 0:
                pl.when(c != pq // 2)(drain)
            else:
                drain()


def in_time_order(landed_ref, out_hbm, result, sems):
    perm = one_hot(TILE, lambda r: ((r >> 2) & 3) * 64 + (r >> 4) * 4 + (r & 3))
    writes = []
    for h in range(4):
        rows = pl.ds(h * TILE, TILE)
        result[rows, :] = jnp.dot(
            perm, landed_ref[h].reshape(TILE, WIDTH), preferred_element_type=F32
        ).astype(BF16)
        writes.append(pltpu.make_async_copy(result.at[rows], out_hbm.at[rows], sems.at[h]))
        writes[-1].start()
    for write in writes:
        write.wait()


def on_device(patches, dest_map, series_ids, lengths, w_qkv, w_out, gain_var, gain_time):
    any_space = pl.BlockSpec(memory_space=pl.ANY)
    landed = pl.pallas_call(
        kernel,
        out_shape=pltpu.VMEM((4, 16, ROW, WIDTH), BF16),
        in_specs=[any_space] * 8,
        out_specs=pl.BlockSpec(memory_space=pltpu.VMEM),
        scratch_shapes=[
            pltpu.VMEM((64, ROW, WIDTH), BF16),
            pltpu.VMEM((8, 64), jnp.int32),
            pltpu.VMEM((2, 1, WIDTH), F32),
            pltpu.VMEM((128, 128), F32),
            pltpu.VMEM((1, 64), jnp.int32),
            pltpu.SMEM((1, 64), jnp.int32),
            pltpu.VMEM((WIDTH, 3 * WIDTH), BF16),
            pltpu.VMEM((WIDTH, WIDTH), BF16),
            pltpu.VMEM((2, 128, 128), F32),
            pltpu.VMEM((3, TILE, TILE), BF16),
            pltpu.VMEM((2, TILE // 2, TILE // 2), BF16),
            pltpu.VMEM((64, ROW, WIDTH), BF16),
            pltpu.VMEM((64, ROW, WIDTH), BF16),
            pltpu.VMEM((2, 512, WIDTH), BF16),
            pltpu.VMEM((2, 512, WIDTH), BF16),
            pltpu.VMEM((4, 4, 4, ROW, WIDTH), BF16),
            pltpu.VMEM((2, 512, WIDTH), BF16),
            pltpu.VMEM((TILE, WIDTH), BF16),
            pltpu.VMEM((TILE, 3 * WIDTH), BF16),
            pltpu.VMEM((2, 512, 3 * WIDTH), BF16),
            pltpu.VMEM((TILE, WIDTH), BF16),
            pltpu.SemaphoreType.DMA((9,)),
            pltpu.SemaphoreType.DMA((3,)),
            pltpu.SemaphoreType.DMA((64,)),
            pltpu.SemaphoreType.DMA((64,)),
            pltpu.SemaphoreType.DMA((2, 3, 8)),
            pltpu.SemaphoreType.DMA((2, 3, 8)),
            pltpu.SemaphoreType.DMA((4, 4)),
            pltpu.SemaphoreType.DMA((16,)),
        ],
        compiler_params=pltpu.CompilerParams(
            collective_id=0, has_side_effects=True, vmem_limit_bytes=52 << 20
        ),
        cost_estimate=pl.CostEstimate(
            flops=20_000_000_000, bytes_accessed=12_000_000, transcendentals=4_000_000
        ),
        name="pack_layer",
    )(
        patches.reshape(64, ROW, WIDTH),
        dest_map,
        series_ids,
        lengths,
        w_qkv,
        w_out,
        gain_var.reshape(1, WIDTH),
        gain_time.reshape(1, WIDTH),
    )
    return pl.pallas_call(
        in_time_order,
        out_shape=jax.ShapeDtypeStruct((1024, WIDTH), BF16),
        in_specs=[pl.BlockSpec(memory_space=pltpu.VMEM)],
        out_specs=any_space,
        scratch_shapes=[pltpu.VMEM((1024, WIDTH), BF16), pltpu.SemaphoreType.DMA((4,))],
        compiler_params=pltpu.CompilerParams(vmem_limit_bytes=8 << 20),
        name="time_order",
    )(landed)


def solution(mesh):
    return jax.shard_map(
        on_device,
        mesh=mesh,
        in_specs=(
            P(("seq", "grp"), None),
            P(("seq", "grp"), None),
            P("seq", None),
            P("seq", None),
            P(),
            P(),
            P(),
            P(),
        ),
        out_specs=P(("seq", "grp"), None),
        check_vma=False,
    )
```

```python
import functools
import math

import jax
import jax.numpy as jnp
from jax import lax
from jax.experimental import pallas as pl
from jax.experimental.pallas import tpu as pltpu
from jax.sharding import PartitionSpec as P

MESH = pl.DeviceIdType.MESH
BF16 = jnp.bfloat16
F32 = jnp.float32

WIDTH = 1024
ROW = 16
TILE = 256
COLS = 512
SCALE = 64**-0.5 * math.log2(math.e)


PARTNERS = ((0, 0), (2, 0), (2, 1), (1, 0), (3, 1), (1, 1), (3, 0), (0, 1))
CHUNKS = ((0, 4), (4, 2), (6, 2))


def hop(e):
    return jnp.where((e & 1) == 1, (e + 1) >> 1, (8 - (e >> 1)) & 7)


def hop_scalar(e):
    return jnp.where(e % 2 == 1, (e + 1) // 2, lax.rem(8 - e // 2, 8))


def one_hot(size, target):
    rows = lax.broadcasted_iota(jnp.int32, (size, size), 0)
    cols = lax.broadcasted_iota(jnp.int32, (1, size), 1)
    return jnp.where(rows == target(cols), 1.0, 0.0).astype(BF16)


def kernel(
    patches_hbm,
    dest_hbm,
    ids_hbm,
    lengths_hbm,
    wqkv_hbm,
    wout_hbm,
    gain_var_hbm,
    gain_time_hbm,
    landed,
    patches,
    small,
    gains,
    info_own,
    order_down,
    order_ref,
    wqkv,
    wout,
    info,
    perms,
    perms_half,
    outgoing,
    packed,
    spread,
    turned,
    back,
    resid,
    normed,
    qkv,
    qkv_time,
    context,
    load_sem,
    info_sem,
    send1,
    recv1,
    send2,
    recv2,
    send3,
    recv3,
):
    seq = lax.axis_index("seq")
    y = lax.axis_index("grp")
    z, x, c = seq // 8, lax.rem(seq // 2, 4), lax.rem(seq, 2)
    chip = z * 4 + x
    to_core = x // 2
    member = y * 2 + c

    loads = [
        pltpu.make_async_copy(patches_hbm, patches, load_sem.at[0]),
        pltpu.make_async_copy(dest_hbm, small.at[pl.ds(2, 1)], load_sem.at[1]),
        pltpu.make_async_copy(ids_hbm, small.at[pl.ds(0, 1)], load_sem.at[2]),
        pltpu.make_async_copy(lengths_hbm, small.at[pl.ds(1, 1)], load_sem.at[3]),
        pltpu.make_async_copy(gain_var_hbm, gains.at[0], load_sem.at[4]),
        pltpu.make_async_copy(gain_time_hbm, gains.at[1], load_sem.at[5]),
        pltpu.make_async_copy(wqkv_hbm, wqkv, load_sem.at[6]),
        pltpu.make_async_copy(wout_hbm, wout, load_sem.at[7]),
    ]
    for load in loads[:4]:
        load.start()

    barrier = pltpu.get_barrier_semaphore()

    @pl.loop(0, 32)
    def _(j):
        source = ((j // 4) * 4 + 2 * c + lax.rem(j // 2, 2)) * 2 + lax.rem(j, 2)

        @pl.when(source != seq)
        def _():
            pl.semaphore_signal(
                barrier, inc=1, device_id={"seq": source, "grp": y}, device_id_type=MESH
            )

    @pl.loop(1, 8)
    def _(j):
        pl.semaphore_signal(
            barrier,
            inc=1,
            device_id={
                "seq": chip * 2 + lax.rem(c + j, 2),
                "grp": lax.rem(y + j // 2, 4),
            },
            device_id_type=MESH,
        )

    eye = lax.broadcasted_iota(jnp.int32, (64, 64), 0) == lax.broadcasted_iota(
        jnp.int32, (64, 64), 1
    )

    def down(row):
        return jnp.sum(jnp.where(eye, row.astype(F32), 0.0), axis=1, keepdims=True)

    loads[1].wait()
    pack = lax.broadcasted_iota(jnp.int32, (64, 64), 1).astype(F32)
    number = lax.broadcasted_iota(jnp.int32, (64, 64), 0)
    order = jnp.sum(
        jnp.where(down(small[2:3, :]) == pack, number, 0), axis=0, keepdims=True
    )
    order_down[...] = jnp.minimum(order, 63)
    to_scalars = pltpu.make_async_copy(order_down, order_ref, load_sem.at[8])
    to_scalars.start()

    pl.semaphore_wait(barrier, 39 - jnp.where(to_core == c, 1, 0))
    to_scalars.wait()
    loads[0].wait()
    for load in loads[4:]:
        load.start()

    def place1(jj):
        e, dx, p = lax.rem(jj // 4, 8), lax.rem(jj, 4), jj // 32
        to_chip = lax.rem(z + hop_scalar(e), 8) * 4 + lax.rem(x + dx, 4)
        slot = p * 32 + e * 4 + lax.rem(x, 2) * 2 + c
        return to_chip, to_chip * 2 + to_core, p, slot

    def send_blocks(begin, end):
        @pl.loop(begin, end)
        def _(jj):
            to_chip, dest, p, slot = place1(jj)
            block = jnp.minimum(order_ref[0, to_chip * 2 + p], 63)
            outgoing[jj] = patches[block]

            @pl.when(dest != seq)
            def _():
                pltpu.make_async_remote_copy(
                    src_ref=outgoing.at[jj],
                    dst_ref=packed.at[slot],
                    send_sem=send1.at[jj],
                    recv_sem=recv1.at[slot],
                    device_id={"seq": dest, "grp": y},
                    device_id_type=MESH,
                ).start()

            @pl.when(dest == seq)
            def _():
                pltpu.make_async_copy(
                    outgoing.at[jj], packed.at[slot], recv1.at[slot]
                ).start()

    send_blocks(0, 64)

    loads[2].wait()
    loads[3].wait()
    ids = small[0:1, :].astype(F32)
    same = jnp.where(down(small[0:1, :]) == ids, 1.0, 0.0)
    info_own[:64, :64] = same
    info_own[:64, 64:] = same
    info_own[64:, :] = jnp.broadcast_to(down(small[1:2, :]), (64, 128))
    info_local = pltpu.make_async_copy(info_own, info.at[c], info_sem.at[0])
    info_remote = pltpu.make_async_remote_copy(
        src_ref=info_own,
        dst_ref=info.at[c],
        send_sem=info_sem.at[1],
        recv_sem=info_sem.at[2],
        device_id={"seq": chip * 2 + 1 - c, "grp": y},
        device_id_type=MESH,
    )
    info_local.start()
    info_remote.start()

    def by_variate(times):
        return lambda r: (r & 63) * times + (r >> 6)

    def gathered(shift):
        return lambda r: (
            (((r >> shift) & 7) << (3 + shift))
            + ((r >> (3 + shift)) << shift)
            + (r & ((1 << shift) - 1))
        )

    def sent(pos):
        early = pos < 32
        e = jnp.where(early, pos & 3, 4 + ((pos >> 4) & 1) * 2 + (pos & 1))
        sender = jnp.where(early, pos >> 2, (pos & 15) >> 1)
        return sender, 2 * ((z - hop(e) + 8) & 7) + (sender & 1)

    def to_time(r):
        sender, k = sent(r & 63)
        return (sender >> 1) * 64 + k * 4 + (r >> 6)

    perms[0] = one_hot(TILE, by_variate(4))
    perms[1] = one_hot(TILE, gathered(2))
    perms[2] = one_hot(TILE, to_time)
    perms_half[0] = one_hot(TILE // 2, by_variate(2))
    perms_half[1] = one_hot(TILE // 2, gathered(1))

    lanes = lax.broadcasted_iota(jnp.int32, (64, 128), 1)
    first_half = lanes < 64
    diag_rows = lax.broadcasted_iota(jnp.int32, (128, 128), 0) // 64
    diag_cols = lax.broadcasted_iota(jnp.int32, (128, 128), 1) // 64
    ones = jnp.where(diag_rows == diag_cols, 1.0, 0.0).astype(BF16)
    key_sender, key_k = sent(lanes & 63)
    key_time = (16 * (key_sender >> 1) + key_k).astype(F32)

    def norm(rows, gain):
        size = rows.shape[0]
        wide = rows.astype(F32)
        mean = jnp.sum(wide * wide, axis=-1, keepdims=True) * (1.0 / WIDTH)
        normed[:size] = (wide * lax.rsqrt(mean + 1e-05) * gains[gain]).astype(BF16)

    zero = jnp.zeros((64, 128), BF16)

    def apart(pair):
        return jnp.concatenate(
            [jnp.where(first_half, pair, zero), jnp.where(first_half, zero, pair)], 0
        )

    def attend(source, begin, keeps):
        parts = [(u, pair * 128) for u in range(len(keeps)) for pair in range(8)]
        expos = []
        scored = []
        for u, col in parts:
            rows = slice(begin + u * 64, begin + u * 64 + 64)
            scores = lax.dot_general(
                source[rows, col : col + 128],
                apart(source[rows, WIDTH + col : WIDTH + col + 128]),
                (((1,), (1,)), ((), ())),
                preferred_element_type=F32,
            )
            scored.append(jnp.where(keeps[u], scores, -1e30))
        for scores in scored:
            low = jnp.max(jnp.where(first_half, scores, -jnp.inf), axis=-1, keepdims=True)
            high = jnp.max(jnp.where(first_half, -jnp.inf, scores), axis=-1, keepdims=True)
            expos.append(
                jnp.exp2((scores - jnp.where(first_half, low, high)) * SCALE).astype(BF16)
            )
        for (u, col), expo in zip(parts, expos):
            rows = slice(begin + u * 64, begin + u * 64 + 64)
            values = apart(source[rows, 2 * WIDTH + col : 2 * WIDTH + col + 128])
            both = jnp.dot(
                expo, jnp.concatenate([values, ones], 1), preferred_element_type=F32
            )
            context[u * 64 : u * 64 + 64, col : col + 128] = (
                both[:, :128] / both[:, 128:]
            ).astype(BF16)

    def variates(p, q):
        begin, count = CHUNKS[q]
        size = count * 64

        @pl.loop(0, count * 4)
        def _(j):
            slot = p * 32 + begin * 4 + j
            pltpu.make_async_copy(packed.at[slot], packed.at[slot], recv1.at[slot]).wait()

        blocks = pl.ds(pl.multiple_of(p * 32 + begin * 4, 4), count * 4)
        norm(packed[blocks].reshape(size, WIDTH), 0)
        for col in range(0, 3 * WIDTH, COLS):
            cols = slice(col, col + COLS)
            qkv[:size, cols] = jnp.dot(
                normed[:size], wqkv[:, cols], preferred_element_type=F32
            ).astype(BF16)
        keep = info[p, :64, :] > 0.5
        attend(qkv, 0, [keep] * count)
        for col in range(0, WIDTH, COLS):
            cols = slice(col, col + COLS)
            normed[:size, cols] = (
                jnp.dot(context[:size], wout[:, cols], preferred_element_type=F32)
                + packed[blocks, :, cols].reshape(size, COLS).astype(F32)
            ).astype(BF16)
        perm = perms[0] if count == 4 else perms_half[0]
        for col in range(0, WIDTH, COLS):
            cols = slice(col, col + COLS)
            spread[p, begin * 64 : begin * 64 + size, cols] = jnp.dot(
                perm, normed[:size, cols], preferred_element_type=F32
            ).astype(BF16)
        part = count * 8
        for j, (dy, dc) in enumerate(PARTNERS):
            dest_y, dest_c = lax.rem(y + dy, 4), lax.rem(c + dc, 2)
            dest = dest_y * 2 + dest_c
            source = spread.at[p, pl.ds(pl.multiple_of(begin * 64 + dest * part, 16), part)]
            target = turned.at[p, pl.ds(pl.multiple_of(begin * 64 + member * part, 16), part)]
            if j == 0:
                pltpu.make_async_copy(source, target, recv2.at[p, q, member]).start()
            else:
                pltpu.make_async_remote_copy(
                    src_ref=source,
                    dst_ref=target,
                    send_sem=send2.at[p, q, j],
                    recv_sem=recv2.at[p, q, member],
                    device_id={"seq": chip * 2 + dest_c, "grp": dest_y},
                    device_id_type=MESH,
                ).start()

    def project_time(p, q):
        begin, count = CHUNKS[q]
        size, part = count * 64, count * 8

        @pl.loop(0, 8)
        def _(j):
            piece = turned.at[p, pl.ds(pl.multiple_of(begin * 64 + j * part, 16), part)]
            pltpu.make_async_copy(piece, piece, recv2.at[p, q, j]).wait()

        perm = perms[1] if count == 4 else perms_half[1]
        rows = jnp.dot(
            perm, turned[p, begin * 64 : begin * 64 + size], preferred_element_type=F32
        ).astype(BF16)
        for v in range(8):
            at = v * 64 + begin * 8
            resid[p, at : at + part, :] = rows[v * part : v * part + part, :]
        norm(rows, 1)
        for col in range(0, 3 * WIDTH, COLS):
            cols = slice(col, col + COLS)
            proj = jnp.dot(
                normed[:size], wqkv[:, cols], preferred_element_type=F32
            ).astype(BF16)
            for v in range(8):
                at = v * 64 + begin * 8
                qkv_time[p, at : at + part, cols] = proj[v * part : v * part + part, :]

    def times(p, h):
        keeps = []
        for u in range(4):
            length = info[p, pl.ds(64 + member * 8 + h * 4 + u, 1), :]
            keeps.append(key_time < jnp.broadcast_to(length, (64, 128)))
        attend(qkv_time.at[p], h * TILE, keeps)
        for col in range(0, WIDTH, COLS):
            cols = slice(col, col + COLS)
            normed[:, cols] = (
                jnp.dot(context[...], wout[:, cols], preferred_element_type=F32)
                + resid[p, h * TILE : h * TILE + TILE, cols].astype(F32)
            ).astype(BF16)
        for col in range(0, WIDTH, COLS):
            cols = slice(col, col + COLS)
            second = jnp.dot(perms[2], normed[:, cols], preferred_element_type=F32).astype(BF16)
            back[2 * p + h, :, :, :, cols] = second.reshape(4, 4, ROW, COLS)

        for j in (2, 1, 3, 0):
            dest_y = lax.rem(y + j, 4)
            source = back.at[2 * p + h, dest_y]
            target = landed.at[:, member * 2 + h]

            def send():
                pltpu.make_async_remote_copy(
                    src_ref=source,
                    dst_ref=target,
                    send_sem=send3.at[2 * p + h, j],
                    recv_sem=recv3.at[member * 2 + h],
                    device_id={"seq": chip * 2 + p, "grp": dest_y},
                    device_id_type=MESH,
                ).start()

            if j == 0:
                pl.when(c != p)(send)

                @pl.when(c == p)
                def _():
                    pltpu.make_async_copy(source, target, recv3.at[member * 2 + h]).start()
            else:
                send()

    for load in loads[4:]:
        load.wait()
    info_local.wait()
    info_remote.wait()

    variates(0, 0)
    project_time(0, 0)
    variates(0, 1)
    variates(0, 2)
    project_time(0, 1)
    project_time(0, 2)
    times(0, 0)
    variates(1, 0)
    variates(1, 1)
    variates(1, 2)
    times(0, 1)
    project_time(1, 0)
    project_time(1, 1)
    project_time(1, 2)
    times(1, 0)
    times(1, 1)

    @pl.loop(0, 16)
    def _(j):
        part = landed.at[:, j]
        pltpu.make_async_copy(part, part, recv3.at[j]).wait()

    @pl.loop(0, 64)
    def _(jj):
        _, dest, _, _ = place1(jj)

        @pl.when(dest != seq)
        def _():
            pltpu.make_async_copy(outgoing.at[jj], outgoing.at[jj], send1.at[jj]).wait()

    for p in range(2):
        for q, (_, count) in enumerate(CHUNKS):
            for j in range(1, 8):
                part = spread.at[p, pl.ds(0, count * 8)]
                pltpu.make_async_copy(part, part, send2.at[p, q, j]).wait()
    for pq in range(4):
        for j in range(4):

            def drain():
                part = back.at[pq, j]
                pltpu.make_async_copy(part, part, send3.at[pq, j]).wait()

            if j == 0:
                pl.when(c != pq // 2)(drain)
            else:
                drain()


def in_time_order(landed_ref, out_hbm, result, sems):
    perm = one_hot(TILE, lambda r: ((r >> 2) & 3) * 64 + (r >> 4) * 4 + (r & 3))
    writes = []
    for h in range(4):
        rows = pl.ds(h * TILE, TILE)
        result[rows, :] = jnp.dot(
            perm, landed_ref[h].reshape(TILE, WIDTH), preferred_element_type=F32
        ).astype(BF16)
        writes.append(pltpu.make_async_copy(result.at[rows], out_hbm.at[rows], sems.at[h]))
        writes[-1].start()
    for write in writes:
        write.wait()


def on_device(patches, dest_map, series_ids, lengths, w_qkv, w_out, gain_var, gain_time):
    any_space = pl.BlockSpec(memory_space=pl.ANY)
    landed = pl.pallas_call(
        kernel,
        out_shape=pltpu.VMEM((4, 16, ROW, WIDTH), BF16),
        in_specs=[any_space] * 8,
        out_specs=pl.BlockSpec(memory_space=pltpu.VMEM),
        scratch_shapes=[
            pltpu.VMEM((64, ROW, WIDTH), BF16),
            pltpu.VMEM((8, 64), jnp.int32),
            pltpu.VMEM((2, 1, WIDTH), F32),
            pltpu.VMEM((128, 128), F32),
            pltpu.VMEM((1, 64), jnp.int32),
            pltpu.SMEM((1, 64), jnp.int32),
            pltpu.VMEM((WIDTH, 3 * WIDTH), BF16),
            pltpu.VMEM((WIDTH, WIDTH), BF16),
            pltpu.VMEM((2, 128, 128), F32),
            pltpu.VMEM((3, TILE, TILE), BF16),
            pltpu.VMEM((2, TILE // 2, TILE // 2), BF16),
            pltpu.VMEM((64, ROW, WIDTH), BF16),
            pltpu.VMEM((64, ROW, WIDTH), BF16),
            pltpu.VMEM((2, 512, WIDTH), BF16),
            pltpu.VMEM((2, 512, WIDTH), BF16),
            pltpu.VMEM((4, 4, 4, ROW, WIDTH), BF16),
            pltpu.VMEM((2, 512, WIDTH), BF16),
            pltpu.VMEM((TILE, WIDTH), BF16),
            pltpu.VMEM((TILE, 3 * WIDTH), BF16),
            pltpu.VMEM((2, 512, 3 * WIDTH), BF16),
            pltpu.VMEM((TILE, WIDTH), BF16),
            pltpu.SemaphoreType.DMA((9,)),
            pltpu.SemaphoreType.DMA((3,)),
            pltpu.SemaphoreType.DMA((64,)),
            pltpu.SemaphoreType.DMA((64,)),
            pltpu.SemaphoreType.DMA((2, 3, 8)),
            pltpu.SemaphoreType.DMA((2, 3, 8)),
            pltpu.SemaphoreType.DMA((4, 4)),
            pltpu.SemaphoreType.DMA((16,)),
        ],
        compiler_params=pltpu.CompilerParams(
            collective_id=0, has_side_effects=True, vmem_limit_bytes=52 << 20
        ),
        cost_estimate=pl.CostEstimate(
            flops=20_000_000_000, bytes_accessed=12_000_000, transcendentals=4_000_000
        ),
        name="pack_layer",
    )(
        patches.reshape(64, ROW, WIDTH),
        dest_map,
        series_ids,
        lengths,
        w_qkv,
        w_out,
        gain_var.reshape(1, WIDTH),
        gain_time.reshape(1, WIDTH),
    )
    return pl.pallas_call(
        in_time_order,
        out_shape=jax.ShapeDtypeStruct((1024, WIDTH), BF16),
        in_specs=[pl.BlockSpec(memory_space=pltpu.VMEM)],
        out_specs=any_space,
        scratch_shapes=[pltpu.VMEM((1024, WIDTH), BF16), pltpu.SemaphoreType.DMA((4,))],
        compiler_params=pltpu.CompilerParams(vmem_limit_bytes=8 << 20),
        name="time_order",
    )(landed)


def solution(mesh):
    return jax.shard_map(
        on_device,
        mesh=mesh,
        in_specs=(
            P(("seq", "grp"), None),
            P(("seq", "grp"), None),
            P("seq", None),
            P("seq", None),
            P(),
            P(),
            P(),
            P(),
        ),
        out_specs=P(("seq", "grp"), None),
        check_vma=False,
    )
```
